512 devices in a mesh: fsdp: 64 (over y, z_hi, core), tp: 8 (over x, z_lo).
Axes of the slice: x: 4, y: 8, z: 8 (z_hi: 4, z_lo: 2; z = z_hi * 2 + z_lo), core: 2. Of those that a mesh axis runs over, the one named last changes fastest.
Arguments:
- tokens: bfloat16 [8192, 4096], P('fsdp'), may hold values from -16 to 16
- gate_pre: bfloat16 [8192, 14784], P('fsdp', 'tp'), may hold values from -8 to 8
- hid_grad: bfloat16 [8192, 14784], P('fsdp', 'tp'), may hold values from -6 to 6
- up_weight: bfloat16 [4096, 14784], P('fsdp', 'tp'), may hold values from -0.046875 to 0.046875
- grad_accum: float32 [4096, 14784], P('fsdp', 'tp'), may hold values from -6 to 6
Outputs:
- weight_grad: float32 [4096, 14784], P('fsdp', 'tp')
- input_grad: bfloat16 [8192, 4096], P('fsdp', 'tp')
The draws below stay inside these ranges and needn't reach their ends.
All inputs are finite; a program needn't handle non-finite values.
Results may differ from the reference program's by a relative error of at most 0.017.
Values may be sent and summed in bfloat16 or wider, within the bound.
A program may use at most 192 MiB of HBM per device.

```python
import math
import jax
import jax.numpy as jnp
from jax import lax

FF = 14784
DBLK = 4096
TOKENS = 8192
N_TP = 8


def strengthened(values, key, source, target, parts, factor):
    owner, partner = [(jnp.arange(values.shape[axis_at]) // (values.shape[axis_at] // parts)).reshape([-1 if axis == axis_at else 1 for axis in range(values.ndim)]) for axis_at in (source, target)]
    chosen = jax.random.permutation(key, parts)[partner]
    strong = (owner == chosen) | (owner == (partner + parts // 2) % parts)
    return jnp.where(strong, factor * values, values)


def steps_of(rng, dims, split, least, top_value):
    gain, own = 1.0, jax.random.fold_in(rng, 6)
    for position, shards_of in split:
        draws = jnp.exp(jax.random.uniform(jax.random.fold_in(own, position), (shards_of,), jnp.float32, least / len(split), top_value / len(split)))
        gain = gain * jnp.repeat(draws, dims[position] // shards_of).reshape([-1 if axis == position else 1 for axis in range(len(dims))])
    return gain


def centred(rng, dims, deviation, most, shards=(), kind=jnp.bfloat16):
    entries = jax.random.normal(rng, dims, jnp.float32) * deviation
    if len(shards) > 0:
        entries = steps_of(rng, dims, shards, -0.22, 0.18) * entries
    return jnp.clip(entries, min=-most, max=most).astype(kind)


def noise_with(rng, shape, spread, most, split, heavy, held_as=jnp.bfloat16):
    entries = spread * jax.random.normal(rng, shape, jnp.float32)
    if split:
        entries = entries * steps_of(rng, shape, split, -0.22, 0.18)
    return jnp.clip(strengthened(entries, jax.random.fold_in(rng, 3), *heavy), -most, most).astype(held_as)


def setup_inputs(seed: int = 0) -> dict:
    key_list = jax.random.split(jax.random.key(seed), 6)
    tokens = noise_with(key_list[0], (TOKENS, DBLK), 1.0, 16.0, ((0, 64),), (0, 1, 64, 4.0))
    gate_pre = centred(key_list[1], (TOKENS, FF), 1.5, 8.0, ((0, 64), (1, 8)))
    hid_grad = centred(key_list[2], (TOKENS, FF), 1.0, 6.0, ((0, 64), (1, 8)))
    up_weight = centred(key_list[3], (DBLK, FF), FF ** -0.5, 0.046875, ((0, 64), (1, 8)))
    grad_accum = centred(key_list[4], (DBLK, FF), 1.0, 6.0, ((0, 64), (1, 8)), jnp.float32)
    return {"tokens": tokens, "gate_pre": gate_pre, "hid_grad": hid_grad, "up_weight": up_weight, "grad_accum": grad_accum}


def reference(tokens, gate_pre, hid_grad, up_weight, grad_accum):
    gate_value = gate_pre.astype(jnp.float32)
    up_grad = (hid_grad.astype(jnp.float32) * jax.nn.silu(gate_value)).astype(jnp.bfloat16)
    block_grad = lax.dot_general(tokens, up_grad, (((0,), (0,)), ((), ())), preferred_element_type=jnp.float32)
    weight_grad = grad_accum + block_grad * (1.0 / math.sqrt(TOKENS))
    width = FF // N_TP
    summed = jnp.zeros((TOKENS, DBLK), jnp.float32)
    for shard in range(N_TP):
        grad_part = up_grad[:, shard * width:(shard + 1) * width]
        weight_part = up_weight[:, shard * width:(shard + 1) * width]
        partial_value = lax.dot_general(grad_part, weight_part, (((1,), (1,)), ((), ())), preferred_element_type=jnp.float32)
        summed = summed + partial_value.astype(jnp.bfloat16).astype(jnp.float32)
    return (weight_grad, summed.astype(jnp.bfloat16))
```

```python
import math

import jax
import jax.numpy as jnp
from jax import lax
from jax.sharding import Mesh, PartitionSpec as P


def on_device(tokens, gate_pre, hid_grad, up_weight, grad_accum):
    up_grad = (hid_grad.astype(jnp.float32) * jax.nn.silu(gate_pre.astype(jnp.float32))).astype(
        jnp.bfloat16
    )
    n_y, n_zc, n_tp = (lax.axis_size(a) for a in ("y", "zc", "tp"))
    norm_factor = 1.0 / math.sqrt(tokens.shape[0] * n_y * n_zc)
    rows, channels = tokens.shape
    block = channels // n_y
    tok = lax.all_to_all(tokens.reshape(rows, n_y, block), "y", 1, 0, tiled=True)
    tok = tok.reshape(rows * n_y, block)
    ups = lax.all_gather(up_grad, "y", axis=0, tiled=True)
    weight = lax.all_gather(up_weight, "zc", axis=0, tiled=True)
    partial_value = lax.dot_general(
        ups, weight, (((1,), (1,)), ((), ())), preferred_element_type=jnp.float32
    ).astype(jnp.bfloat16)
    summed_input = lax.psum_scatter(partial_value, "tp", scatter_dimension=0, tiled=True)
    input_grad = lax.ppermute(
        summed_input,
        ("y", "tp"),
        [(y * n_tp + t, t * n_tp + y) for y in range(n_y) for t in range(n_tp)],
    )
    complete = lax.dot_general(
        tok, ups, (((0,), (0,)), ((), ())), preferred_element_type=jnp.float32
    ).astype(jnp.bfloat16)
    summed_grad = lax.psum_scatter(complete, "zc", scatter_dimension=0, tiled=True)
    weight_grad = grad_accum + summed_grad.astype(jnp.float32) * norm_factor
    return (weight_grad, input_grad)


def solution(mesh):
    fine = Mesh(mesh.devices.reshape(8, 8, 8), ("y", "zc", "tp"))
    rows, both = P(("y", "zc"), None), P(("y", "zc"), "tp")
    return jax.shard_map(
        on_device,
        mesh=fine,
        in_specs=(rows, both, both, both, both),
        out_specs=(both, both),
        check_vma=False,
    )
```

```python
import functools
import math

import jax
import jax.numpy as jnp
from jax import lax
from jax.experimental import pallas as pl
from jax.experimental.pallas import tpu as pltpu
from jax.sharding import Mesh, PartitionSpec as P

NY, NH, NC, NX, NL = 8, 4, 2, 4, 2
OFF = (0, 1, -1, 2, -2, 3, -3, 4)
BACK = (0, 2, 1, 4, 3, 6, 5, 7)
GROUPS = ((0, 1, 2), (3, 4), (5, 6), (7,))
F32, BF16 = jnp.float32, jnp.bfloat16


def chunks_of(width):
    starts = list(range(0, width, 512))
    return [(s, min(512, width - s)) for s in starts]


def kernel(norm, chunks, n_copies, tokens, gate, hid, w_own, accum, wg_out, ig_out, *scratch):
    scratch = list(scratch)
    take = lambda n: [scratch.pop(0) for _ in range(n)]
    nk = len(chunks)
    send_sem, recv_sem, fin_send, fin_recv = take(4)
    tok, tok_t, w_all, fin = take(4)
    up = take(nk)
    b_send, b_recv, b_own, b_sum = take(nk), take(nk), take(nk), take(nk)
    b_a, b_b, b_tp, b_tm, b_l, b_r = (take(nk) for _ in range(6))
    ng = len(GROUPS)
    p_all, p_a, p_b, p_tp, p_tm, p_l, p_r = (take(ng) for _ in range(7))
    p_sum, p_half, p_z, p_fin = (take(ng) for _ in range(4))

    y, zh, c, x, zl = (lax.axis_index(a) for a in ("y", "zh", "c", "x", "zl"))
    zc, t = zh * NC + c, x * NL + zl
    around = lambda v, n: lax.rem(v + n, n)
    y_up, y_down = {"y": around(y + 1, NY)}, {"y": around(y - 1, NY)}
    h_up, h_down = around(zh + 1, NH), around(zh - 1, NH)
    h_far = around(zh + 2, NH)
    x_up, x_down, x_far = around(x + 1, NX), around(x - 1, NX), around(x + 2, NX)
    sib, pair = {"c": 1 - c}, {"zl": 1 - zl}
    fin_x, fin_l = y // NL, lax.rem(y, NL)

    copies = []

    def send(src, dst, device):
        i = len(copies)
        copy = pltpu.make_async_remote_copy(
            src_ref=src,
            dst_ref=dst,
            send_sem=send_sem.at[i],
            recv_sem=recv_sem.at[i],
            device_id=device,
            device_id_type=pl.DeviceIdType.MESH,
        )
        copy.start()
        copies.append(copy)
        return copy

    def fin_copy(j, src, sem):
        return pltpu.make_async_remote_copy(
            src_ref=src,
            dst_ref=fin.at[x, zl],
            send_sem=fin_send.at[j],
            recv_sem=fin_recv.at[sem],
            device_id={"y": around(y + OFF[j], NY), "x": fin_x, "zl": fin_l},
            device_id_type=pl.DeviceIdType.MESH,
        )

    barrier = pltpu.get_barrier_semaphore()

    def greet(device):
        pl.semaphore_signal(
            barrier, inc=1, device_id=device, device_id_type=pl.DeviceIdType.MESH
        )

    for j in range(1, NY):
        greet({"y": around(y + OFF[j], NY)})
    for device in ({"zh": h_up}, {"zh": h_down}, {"x": x_up}, {"x": x_down}, sib, pair):
        greet(device)
    for other in range(NX * NL):

        @pl.when(jnp.logical_or(t != y, t != other))
        def _():
            greet({"y": t, "x": other // NL, "zl": other % NL})

    def up_grad(k):
        at, width = chunks[k]
        v = gate[:, at : at + width].astype(F32)
        g = hid[:, at : at + width].astype(F32)
        up[k][0] = (g * (v / (1.0 + jnp.exp(-v)))).astype(BF16)

    up_grad(0)
    pl.semaphore_wait(barrier, NY - 1 + 6 + jnp.where(t == y, NX * NL - 1, NX * NL))

    ring = {}
    PLUS, MINUS = (0, 2, 4, 6, 7), (0, 1, 3, 5, 7)

    def pass_on(k, s):
        for way, path, device in ((0, PLUS, y_up), (1, MINUS, y_down)):
            src, dst = up[k].at[path[s]], up[k].at[path[s + 1]]
            if s == 3:
                half = pl.ds(way * 64, 64)
                src, dst = src.at[half], dst.at[half]
            ring[k, s, way] = send(src, dst, device)

    def arrived(k, s):
        for way in (0, 1):
            ring[k, s - 1, way].wait_recv()

    pass_on(0, 0)

    tok_in = []
    for j in range(1, NY):
        to = around(y + OFF[j], NY)
        tok_in.append(
            send(
                tokens.at[
                    pl.ds(pl.multiple_of(x * 32, 32), 32), pl.ds(pl.multiple_of(to * 512, 512), 512)
                ],
                tok.at[BACK[j], x],
                {"y": to},
            )
        )
    w_in = [send(w_own, w_all.at[zc], device) for device in ({"zh": h_up}, {"zh": h_down}, sib)]

    up_grad(1)
    pass_on(1, 0)
    up_grad(2)
    up_grad(3)
    w_all[zc] = w_own[...]

    def w_forward():
        w_in[0].wait_recv()
        w_in[1].wait_recv()
        left, right = h_down * NC + c, h_up * NC + c
        a, b = pl.ds(0, 32), pl.ds(32, 32)
        w_in.append(send(w_all.at[left, a], w_all.at[left, a], {"zh": h_up}))
        w_in.append(send(w_all.at[right, b], w_all.at[right, b], {"zh": h_down}))
        w_in.append(send(w_all.at[left], w_all.at[left], sib))
        w_in.append(send(w_all.at[right], w_all.at[right], sib))

    def w_share():
        far = h_far * NC + c
        w_in[3].wait_recv()
        w_in.append(send(w_all.at[far, pl.ds(0, 32)], w_all.at[far, pl.ds(0, 32)], sib))
        w_in[4].wait_recv()
        w_in.append(send(w_all.at[far, pl.ds(32, 32)], w_all.at[far, pl.ds(32, 32)], sib))

    others = pl.ds(1, NY - 1)
    tok_x = []

    def tok_spread():
        for copy in tok_in:
            copy.wait_recv()
        quarter = tok.at[others, x]
        tok_x.append(send(quarter, quarter, {"x": x_up}))
        tok_x.append(send(quarter, quarter, {"x": x_down}))

    def tok_forward():
        tok_x[0].wait_recv()
        tok_x[1].wait_recv()
        a = tok.at[others, x_down, pl.ds(0, 16)]
        b = tok.at[others, x_up, pl.ds(16, 16)]
        tok_x.append(send(a, a, {"x": x_up}))
        tok_x.append(send(b, b, {"x": x_down}))

    def tok_turn():
        tok_x[2].wait_recv()
        tok_x[3].wait_recv()
        for j in range(NY):
            if j == 0:
                block = tokens[:, pl.ds(pl.multiple_of(y * 512, 512), 512)]
            else:
                block = tok[j].reshape(128, 512)
            turned = block.T
            for h in range(NH):
                for core in range(NC):
                    row = (h * NC + core) * 64
                    tok_t[core, h * 64 : h * 64 + 64, j * 128 : j * 128 + 128] = turned[row : row + 64]

    share = {}
    rs = {}

    def grad_part(k, core):
        ups = up[k][...].reshape(NY * 128, chunks[k][1])
        part = jnp.dot(tok_t[core], ups, preferred_element_type=F32)
        return part.reshape(NH, 64, chunks[k][1])

    def grad_other(k):
        b_send[k][...] = grad_part(k, 1 - c).astype(BF16)
        share[k] = send(b_send[k], b_recv[k], sib)

    def grad_own(k):
        b_own[k][...] = grad_part(k, c)

    def z1(k):
        share[k].wait_recv()
        total = b_own[k][...] + b_recv[k][...].astype(F32)
        b_own[k][...] = total
        b_sum[k][...] = total.astype(BF16)
        rs[k] = [
            send(b_sum[k].at[h_far, pl.ds(0, 32)], b_a[k], {"zh": h_up}),
            send(b_sum[k].at[h_far, pl.ds(32, 32)], b_b[k], {"zh": h_down}),
        ]

    def z2(k):
        rs[k][0].wait_recv()
        b_tp[k][0:32] = (b_own[k][h_up, 0:32] + b_a[k][...].astype(F32)).astype(BF16)
        b_tp[k][32:64] = b_own[k][h_up, 32:64].astype(BF16)
        rs[k].append(send(b_tp[k], b_l[k], {"zh": h_up}))
        rs[k][1].wait_recv()
        b_tm[k][0:32] = b_own[k][h_down, 0:32].astype(BF16)
        b_tm[k][32:64] = (b_own[k][h_down, 32:64] + b_b[k][...].astype(F32)).astype(BF16)
        rs[k].append(send(b_tm[k], b_r[k], {"zh": h_down}))

    def z3(k):
        rs[k][2].wait_recv()
        rs[k][3].wait_recv()
        total = b_own[k][zh] + b_l[k][...].astype(F32) + b_r[k][...].astype(F32)
        at, width = chunks[k]
        wg_out[:, at : at + width] = accum[:, at : at + width] + total * norm

    px = {}

    def partial(g):
        first, n = GROUPS[g][0], len(GROUPS[g])
        total = None
        for k, (at, width) in enumerate(chunks):
            lhs = up[k][first : first + n].reshape(n * 128, width)
            rhs = w_all[:, :, at : at + width].reshape(NH * NC * 64, width)
            term = lax.dot_general(
                lhs, rhs, (((1,), (1,)), ((), ())), preferred_element_type=F32
            )
            total = term if total is None else total + term
        p_all[g][...] = total.astype(BF16).reshape(n, NX, 32, 512)
        px[g] = [
            send(p_all[g].at[:, x_far, pl.ds(0, 16)], p_a[g], {"x": x_up}),
            send(p_all[g].at[:, x_far, pl.ds(16, 16)], p_b[g], {"x": x_down}),
        ]

    def x2(g):
        px[g][0].wait_recv()
        p_tp[g][:, 0:16] = (p_all[g][:, x_up, 0:16].astype(F32) + p_a[g][...].astype(F32)).astype(BF16)
        p_tp[g][:, 16:32] = p_all[g][:, x_up, 16:32]
        px[g].append(send(p_tp[g], p_l[g], {"x": x_up}))
        px[g][1].wait_recv()
        p_tm[g][:, 0:16] = p_all[g][:, x_down, 0:16]
        p_tm[g][:, 16:32] = (
            p_all[g][:, x_down, 16:32].astype(F32) + p_b[g][...].astype(F32)
        ).astype(BF16)
        px[g].append(send(p_tm[g], p_r[g], {"x": x_down}))

    def x3(g):
        px[g][2].wait_recv()
        px[g][3].wait_recv()
        total = p_all[g][:, x].astype(F32) + p_l[g][...].astype(F32) + p_r[g][...].astype(F32)
        n = len(GROUPS[g])
        total = total.reshape(n, NL, 16, 512)
        p_sum[g][...] = total
        p_half[g][...] = total.astype(BF16)
        px[g].append(send(p_half[g].at[:, 1 - zl], p_z[g], pair))

    def x4(g):
        px[g][4].wait_recv()
        p_fin[g][...] = (p_sum[g][:, zl] + p_z[g][...].astype(F32)).astype(BF16)
        for i, j in enumerate(GROUPS[g]):
            if j == 0:

                @pl.when(t == y)
                def _():
                    fin[x, zl] = p_fin[g][i]

                @pl.when(t != y)
                def _():
                    fin_copy(j, p_fin[g].at[i], t).start()

            else:
                fin_copy(j, p_fin[g].at[i], t).start()

    arrived(0, 1); pass_on(0, 1)
    arrived(1, 1); pass_on(1, 1)
    w_forward()
    arrived(0, 2); pass_on(0, 2); pass_on(2, 0)
    tok_spread()
    arrived(0, 3); pass_on(0, 3)
    w_share()
    arrived(1, 2); pass_on(1, 2)
    tok_forward()
    arrived(2, 1); pass_on(2, 1)
    arrived(0, 4)
    tok_turn()
    grad_other(0); grad_own(0)
    arrived(1, 3); pass_on(1, 3); pass_on(3, 0)
    arrived(2, 2); pass_on(2, 2)
    z1(0)
    arrived(3, 1); pass_on(3, 1)
    arrived(1, 4)
    grad_other(1); grad_own(1)
    z2(0)
    arrived(2, 3); pass_on(2, 3)
    z1(1)
    z3(0)
    w_in[2].wait_recv()
    for copy in w_in[5:]:
        copy.wait_recv()
    arrived(3, 2); pass_on(3, 2)
    partial(0)
    z2(1)
    arrived(2, 4)
    grad_other(2); grad_own(2)
    arrived(3, 3); pass_on(3, 3)
    partial(1)
    x2(0)
    z1(2)
    partial(2)
    x2(1)
    x3(0)
    z3(1)
    arrived(3, 4)
    grad_other(3)
    partial(3)
    grad_own(3)
    z2(2)
    x2(2)
    x3(1)
    x4(0)
    z1(3)
    x2(3)
    x3(2)
    x4(1)
    z2(3)
    x3(3)
    x4(2)
    z3(2)
    x4(3)
    z3(3)

    for other in range(NX * NL):

        @pl.when(jnp.logical_or(t != y, t != other))
        def _():
            fin_copy(0, p_fin[0].at[0], other).wait_recv()

    ig_out[...] = fin[...].reshape(128, 512)
    for copy in copies:
        copy.wait_send()
    assert len(copies) == n_copies

    @pl.when(t != y)
    def _():
        fin_copy(0, p_fin[0].at[0], t).wait_send()

    for g, group in enumerate(GROUPS):
        for i, j in enumerate(group):
            if j:
                fin_copy(j, p_fin[g].at[i], t).wait_send()


def on_device(tokens, gate_pre, hid_grad, up_weight, grad_accum):
    rows, channels = tokens.shape
    w_rows, width = up_weight.shape
    norm = 1.0 / math.sqrt(rows * NY * NH * NC)
    chunks = chunks_of(width)
    n_copies = 8 * len(chunks) + 7 + 4 + 9 + 5 * len(chunks) + 5 * len(GROUPS)
    dma, vmem = pltpu.SemaphoreType.DMA, pltpu.VMEM
    widths = [w for _, w in chunks]
    sizes = [len(g) for g in GROUPS]
    scratch = [dma((n_copies,)), dma((n_copies,)), dma((NY,)), dma((NX * NL,))]
    scratch += [
        vmem((NY, NX, 32, 512), BF16),
        vmem((NC, 256, 1024), BF16),
        vmem((NH * NC, w_rows, width), BF16),
        vmem((NX, NL, 16, 512), BF16),
    ]
    scratch += [vmem((NY, rows, w), BF16) for w in widths]
    for shape, kind in (
        ((NH, 64), BF16), ((NH, 64), BF16), ((NH, 64), F32), ((NH, 64), BF16),
        ((32,), BF16), ((32,), BF16), ((64,), BF16), ((64,), BF16), ((64,), BF16), ((64,), BF16),
    ):
        scratch += [vmem((*shape, w), kind) for w in widths]
    for shape, kind in (
        ((NX, 32, 512), BF16), ((16, 512), BF16), ((16, 512), BF16), ((32, 512), BF16),
        ((32, 512), BF16), ((32, 512), BF16), ((32, 512), BF16),
        ((NL, 16, 512), F32), ((NL, 16, 512), BF16), ((16, 512), BF16), ((16, 512), BF16),
    ):
        scratch += [vmem((n, *shape), kind) for n in sizes]
    return pl.pallas_call(
        functools.partial(kernel, norm, chunks, n_copies),
        out_shape=(
            jax.ShapeDtypeStruct((w_rows, width), F32),
            jax.ShapeDtypeStruct((rows, channels // NY), BF16),
        ),
        in_specs=[pl.BlockSpec(memory_space=pltpu.VMEM)] * 5,
        out_specs=(pl.BlockSpec(memory_space=pltpu.VMEM),) * 2,
        scratch_shapes=scratch,
        compiler_params=pltpu.CompilerParams(
            collective_id=0, has_side_effects=True, vmem_limit_bytes=48 * 1024 * 1024
        ),
    )(tokens, gate_pre, hid_grad, up_weight, grad_accum)


def solution(mesh):
    fine = Mesh(mesh.devices.reshape(NY, NH, NC, NX, NL), ("y", "zh", "c", "x", "zl"))
    fsdp = ("y", "zh", "c")
    rows, both = P(fsdp, None), P(fsdp, ("x", "zl"))
    return jax.shard_map(
        on_device,
        mesh=fine,
        in_specs=(rows, both, both, both, both),
        out_specs=(both, both),
        check_vma=False,
    )
```

```python
import functools
import math

import jax
import jax.numpy as jnp
from jax import lax
from jax.experimental import pallas as pl
from jax.experimental.pallas import tpu as pltpu
from jax.sharding import Mesh, PartitionSpec as P

NY, NH, NC, NX, NL = 8, 4, 2, 4, 2
OFF = (0, 1, -1, 2, -2, 3, -3, 4)
BACK = (0, 2, 1, 4, 3, 6, 5, 7)
PLUS, MINUS = (0, 2, 4, 6, 7), (0, 1, 3, 5, 7)
TEAMS = ((0,), (1, 2), (3, 4), (5, 6), (7,))
SPLIT = (640, 1152, 1536)
F32, BF16 = jnp.float32, jnp.bfloat16
PLAN = (
    ("up", 0), ("enter",), ("ring", 0, 0, 0), ("w_send",), ("up", 1), ("ring", 1, 0, 0), ("up", 2),
    ("tok_send",), ("ring", 1, 1, 0), ("ring", 0, 1, 0), ("ring", 0, 0, 1), ("tok_pair",),
    ("ring", 1, 1, 1), ("ring", 1, 0, 1), ("up", 3), ("ring", 0, 1, 1), ("ring", 0, 0, 2),
    ("w_forward",), ("tok_spread",), ("ring", 1, 0, 2), ("ring", 0, 1, 2), ("ring", 2, 1, 0),
    ("ring", 0, 0, 3), ("ring", 2, 0, 0), ("tok_forward",), ("ring", 0, 1, 3), ("ring", 1, 1, 2),
    ("w_share",), ("ring", 3, 0, 0), ("ring", 2, 1, 1), ("ring", 3, 1, 0), ("w_ready",),
    ("p_begin", 0), ("ring", 2, 0, 1), ("got", 0, 0, 4), ("ring", 1, 0, 3), ("p_begin", 1),
    ("got", 0, 1, 4), ("tok_turn",), ("grad_other", 0), ("p_send", 0), ("ring", 1, 1, 3),
    ("ring", 3, 0, 1), ("grad_own", 0), ("ring", 2, 1, 2), ("z_send", 0), ("ring", 3, 1, 1),
    ("p_send", 1), ("ring", 2, 0, 2), ("p_begin", 2), ("got", 1, 0, 4), ("ring", 3, 0, 2),
    ("got", 1, 1, 4), ("grad_other", 1), ("grad_own", 1), ("ring", 2, 1, 3), ("ring", 3, 1, 2),
    ("p_send", 2), ("ring", 2, 0, 3), ("z_send", 1), ("ring", 3, 0, 3), ("p_begin", 3),
    ("ring", 3, 1, 3), ("got", 2, 1, 4), ("p_send", 3), ("got", 2, 0, 4), ("grad_other", 2),
    ("grad_own", 2), ("p_end", 0), ("p_begin", 4), ("got", 3, 0, 4), ("p_end", 1), ("got", 3, 1, 4),
    ("z_send", 2), ("z_end", 0), ("p_end", 2), ("p_send", 4), ("grad_other", 3), ("grad_own", 3),
    ("p_end", 3), ("z_send", 3), ("p_end", 4), ("drain",), ("z_end", 1), ("z_end", 2), ("z_end", 3),
)


def kernel(norm, chunks, n_copies, tokens, gate_in, hid_in, w_own, accum_in, wg_out, ig_out, *scratch):
    scratch = list(scratch)
    take = lambda n: [scratch.pop(0) for _ in range(n)]
    nk = len(chunks)
    send_sem, recv_sem, fin_send, fin_recv, load_sem = take(5)
    gate, hid, accum, wg, ig, tok_own, tok, tok_t, w_all, fin = take(10)
    up = take(nk)
    b_send, b_recv, b_own, b_sum, b_l, b_r, b_f = (take(nk) for _ in range(7))
    nt = len(TEAMS)
    p_acc, p_all, p_l, p_r, p_f, p_fin = (take(nt) for _ in range(6))

    y, zh, c, x, zl = (lax.axis_index(a) for a in ("y", "zh", "c", "x", "zl"))
    zc, t = zh * NC + c, x * NL + zl
    around = lambda v, n: lax.rem(v + n, n)
    y_up, y_down = {"y": around(y + 1, NY)}, {"y": around(y - 1, NY)}
    h_up, h_down = around(zh + 1, NH), around(zh - 1, NH)
    h_far = around(zh + 2, NH)
    x_up, x_down, x_far = around(x + 1, NX), around(x - 1, NX), around(x + 2, NX)
    sib = {"c": 1 - c}
    fin_x, fin_l = y // NL, lax.rem(y, NL)
    MESH = pl.DeviceIdType.MESH

    copies = []

    def send(src, dst, device):
        i = len(copies)
        copy = pltpu.make_async_remote_copy(
            src_ref=src,
            dst_ref=dst,
            send_sem=send_sem.at[i],
            recv_sem=recv_sem.at[i],
            device_id=device,
            device_id_type=MESH,
        )
        copy.start()
        copies.append(copy)
        return copy

    def fin_copy(j, src, sem):
        return pltpu.make_async_remote_copy(
            src_ref=src,
            dst_ref=fin.at[x, zl],
            send_sem=fin_send.at[j],
            recv_sem=fin_recv.at[sem],
            device_id={"y": around(y + OFF[j], NY), "x": fin_x, "zl": fin_l},
            device_id_type=MESH,
        )

    barrier = pltpu.get_barrier_semaphore()

    def greet(device):
        pl.semaphore_signal(barrier, inc=1, device_id=device, device_id_type=MESH)

    for j in range(1, NY):
        greet({"y": around(y + OFF[j], NY)})
    for h in (h_up, h_down, h_far):
        greet({"zh": h})
    for v in (x_up, x_down, x_far):
        greet({"x": v})
    greet({"zl": 1 - zl})
    greet(sib)
    for other in range(NX * NL):

        @pl.when(jnp.logical_or(t != y, t != other))
        def _():
            greet({"y": t, "x": other // NL, "zl": other % NL})

    loads = {}

    def load(name, src, dst):
        loads[name] = pltpu.make_async_copy(src, dst, load_sem.at[len(loads)])
        loads[name].start()

    for k, (at, width) in enumerate(chunks):
        part = pl.ds(at, width)
        load((0, k), gate_in.at[part], gate.at[part])
        load((1, k), hid_in.at[part], hid.at[part])

    def load_rest():
        load("w", w_own, w_all.at[zc])
        columns = pl.ds(pl.multiple_of(y * 512, 512), 512)
        load("tok", tokens.at[:, columns], tok_own)
        load("accum", accum_in, accum)

    def up_grad(k):
        loads[0, k].wait()
        loads[1, k].wait()
        at, width = chunks[k]
        v = gate[at : at + width].astype(F32)
        g = hid[at : at + width].astype(F32)
        up[k][0] = (g * (v / (1.0 + jnp.exp(-v)))).astype(BF16).T

    ring = {}

    def arrived(k, half, s):
        for way in (0, 1):
            if s < 4 or way == half:
                ring[k, half, s - 1, way].wait_recv()

    def ring_step(k, half, s):
        if s:
            arrived(k, half, s)
        rows = pl.ds(half * 64, 64)
        for way, path, device in ((0, PLUS, y_up), (1, MINUS, y_down)):
            if s < 3 or way == half:
                ring[k, half, s, way] = send(
                    up[k].at[path[s], rows], up[k].at[path[s + 1], rows], device
                )

    tok_in, tok_x = [], []
    others = pl.ds(1, NY - 1)

    def tok_send():
        for j in range(1, NY):
            to = around(y + OFF[j], NY)
            rows = pl.ds(pl.multiple_of(t * 16, 16), 16)
            columns = pl.ds(pl.multiple_of(to * 512, 512), 512)
            tok_in.append(send(tokens.at[rows, columns], tok.at[BACK[j], x, zl], {"y": to}))

    def tok_pair():
        for copy in tok_in:
            copy.wait_recv()
        eighth = tok.at[others, x, zl]
        tok_in.append(send(eighth, eighth, {"zl": 1 - zl}))

    def tok_spread():
        tok_in[NY - 1].wait_recv()
        quarter = tok.at[others, x]
        tok_x.append(send(quarter, quarter, {"x": x_up}))
        tok_x.append(send(quarter, quarter, {"x": x_down}))

    def tok_forward():
        tok_x[0].wait_recv()
        tok_x[1].wait_recv()
        a = tok.at[others, x_down, 0]
        b = tok.at[others, x_up, 1]
        tok_x.append(send(a, a, {"x": x_up}))
        tok_x.append(send(b, b, {"x": x_down}))

    def tok_turn():
        tok_x[2].wait_recv()
        tok_x[3].wait_recv()
        for j in range(NY):
            if j == 0:
                loads["tok"].wait()
                block = tok_own[...]
            else:
                block = tok[j].reshape(128, 512)
            turned = block.T
            for h in range(NH):
                for core in range(NC):
                    row = (h * NC + core) * 64
                    tok_t[core, h * 64 : h * 64 + 64, j * 128 : j * 128 + 128] = turned[row : row + 64]

    w_in = []

    def w_send():
        for device in ({"zh": h_up}, {"zh": h_down}, sib):
            w_in.append(send(w_own, w_all.at[zc], device))
        load_rest()

    def w_forward():
        w_in[0].wait_recv()
        w_in[1].wait_recv()
        left, right = h_down * NC + c, h_up * NC + c
        a, b = pl.ds(0, 32), pl.ds(32, 32)
        w_in.append(send(w_all.at[left, a], w_all.at[left, a], {"zh": h_up}))
        w_in.append(send(w_all.at[right, b], w_all.at[right, b], {"zh": h_down}))
        w_in.append(send(w_all.at[left], w_all.at[left], sib))
        w_in.append(send(w_all.at[right], w_all.at[right], sib))

    def w_share():
        far = h_far * NC + c
        w_in[3].wait_recv()
        w_in.append(send(w_all.at[far, pl.ds(0, 32)], w_all.at[far, pl.ds(0, 32)], sib))
        w_in[4].wait_recv()
        w_in.append(send(w_all.at[far, pl.ds(32, 32)], w_all.at[far, pl.ds(32, 32)], sib))

    def w_ready():
        loads["w"].wait()
        w_in[2].wait_recv()
        for copy in w_in[5:]:
            copy.wait_recv()

    share, zs = {}, {}

    def grad_part(k, core):
        ups = up[k][...].reshape(NY * 128, chunks[k][1])
        part = jnp.dot(tok_t[core], ups, preferred_element_type=F32)
        return part.reshape(NH, 64, chunks[k][1])

    def grad_other(k):
        b_send[k][...] = grad_part(k, 1 - c).astype(BF16)
        share[k] = send(b_send[k], b_recv[k], sib)

    def grad_own(k):
        b_own[k][...] = grad_part(k, c)

    def z_send(k):
        share[k].wait_recv()
        total = b_own[k][...] + b_recv[k][...].astype(F32)
        b_own[k][...] = total
        b_sum[k][...] = total.astype(BF16)
        zs[k] = [
            send(b_sum[k].at[h], into[k], {"zh": h})
            for h, into in ((h_far, b_f), (h_up, b_l), (h_down, b_r))
        ]

    def z_end(k):
        for copy in zs[k]:
            copy.wait_recv()
        if k == 0:
            loads["accum"].wait()
        total = b_own[k][zh]
        for other in (b_l, b_r, b_f):
            total = total + other[k][...].astype(F32)
        at, width = chunks[k]
        wg[:, at : at + width] = accum[:, at : at + width] + total * norm
        load((2, k), wg.at[:, pl.ds(at, width)], wg_out.at[:, pl.ds(at, width)])

    xs = {}

    def term(p, ks):
        first, n = TEAMS[p][0], len(TEAMS[p])
        total = None
        for k, cut in [(k, cut) for k in ks for cut in range(0, chunks[k][1], 512)]:
            at, width = chunks[k]
            end = min(cut + 512, width)
            lhs = up[k][first : first + n, :, cut:end].reshape(n * 128, end - cut)
            rhs = w_all[:, :, at + cut : at + end].reshape(NH * NC * 64, end - cut)
            one = lax.dot_general(lhs, rhs, (((1,), (1,)), ((), ())), preferred_element_type=F32)
            total = one if total is None else total + one
        return total

    def p_begin(p):
        p_acc[p][...] = term(p, range(nk - 1))

    def p_send(p):
        total = p_acc[p][...] + term(p, (nk - 1,))
        p_all[p][...] = total.astype(BF16).reshape(len(TEAMS[p]), NX, 32, 512)
        xs[p] = [
            send(p_all[p].at[:, v], into[p], {"x": v})
            for v, into in ((x_far, p_f), (x_up, p_l), (x_down, p_r))
        ]

    def p_end(p):
        for copy in xs[p]:
            copy.wait_recv()
        total = p_all[p][:, x].astype(F32)
        for other in (p_l, p_r, p_f):
            total = total + other[p][...].astype(F32)
        p_fin[p][...] = total.astype(BF16)
        for i, j in enumerate(TEAMS[p]):
            if j == 0:

                @pl.when(t == y)
                def _():
                    fin[x, zl] = p_fin[p][i]

                @pl.when(t != y)
                def _():
                    fin_copy(j, p_fin[p].at[i], t).start()

            else:
                fin_copy(j, p_fin[p].at[i], t).start()

    drained = []

    def drain():
        for copy in copies[len(drained) :]:
            copy.wait_send()
            drained.append(copy)

    def enter():
        pl.semaphore_wait(barrier, NY - 1 + 8 + jnp.where(t == y, NX * NL - 1, NX * NL))

    steps = {
        "enter": enter, "drain": drain, "up": up_grad, "ring": ring_step, "got": arrived,
        "tok_send": tok_send, "tok_pair": tok_pair, "tok_spread": tok_spread, "tok_forward": tok_forward, "tok_turn": tok_turn,
        "w_send": w_send, "w_forward": w_forward, "w_share": w_share, "w_ready": w_ready,
        "grad_other": grad_other, "grad_own": grad_own, "z_send": z_send, "z_end": z_end,
        "p_begin": p_begin, "p_send": p_send, "p_end": p_end,
    }
    for step, *of in PLAN:
        steps[step](*of)

    for other in range(NX * NL):

        @pl.when(jnp.logical_or(t != y, t != other))
        def _():
            fin_copy(0, p_fin[0].at[0], other).wait_recv()

    ig[...] = (fin[:, 0].astype(F32) + fin[:, 1].astype(F32)).astype(BF16).reshape(128, 512)
    load("ig", ig, ig_out)
    drain()
    loads["ig"].wait()
    for k in range(nk):
        loads[2, k].wait()
    assert len(copies) == n_copies

    @pl.when(t != y)
    def _():
        fin_copy(0, p_fin[0].at[0], t).wait_send()

    for p, team in enumerate(TEAMS):
        for i, j in enumerate(team):
            if j:
                fin_copy(j, p_fin[p].at[i], t).wait_send()


def on_device(tokens, gate_pre, hid_grad, up_weight, grad_accum):
    rows, channels = tokens.shape
    w_rows, width = up_weight.shape
    norm = 1.0 / math.sqrt(rows * NY * NH * NC)
    ends = (*SPLIT, width)
    chunks = [(at, end - at) for at, end in zip((0, *SPLIT), ends)]
    n_copies = 14 * len(chunks) + 8 + 4 + 9 + 4 * len(chunks) + 3 * len(TEAMS)
    dma, vmem = pltpu.SemaphoreType.DMA, pltpu.VMEM
    widths = [w for _, w in chunks]
    sizes = [len(team) for team in TEAMS]
    scratch = [dma((n_copies,)), dma((n_copies,)), dma((NY,)), dma((NX * NL,))]
    scratch += [dma((3 * len(chunks) + 4,))]
    scratch += [
        vmem((width, rows), BF16),
        vmem((width, rows), BF16),
        vmem((w_rows, width), F32),
        vmem((w_rows, width), F32),
        vmem((rows, 512), BF16),
        vmem((rows, 512), BF16),
        vmem((NY, NX, NL, 16, 512), BF16),
        vmem((NC, 256, 1024), BF16),
        vmem((NH * NC, w_rows, width), BF16),
        vmem((NX, NL, 32, 512), BF16),
    ]
    scratch += [vmem((NY, rows, w), BF16) for w in widths]
    for shape, kind in (
        ((NH, 64), BF16), ((NH, 64), BF16), ((NH, 64), F32), ((NH, 64), BF16),
        ((64,), BF16), ((64,), BF16), ((64,), BF16),
    ):
        scratch += [vmem((*shape, w), kind) for w in widths]
    scratch += [vmem((n * 128, 512), F32) for n in sizes]
    scratch += [vmem((n, NX, 32, 512), BF16) for n in sizes]
    for _ in range(4):
        scratch += [vmem((n, 32, 512), BF16) for n in sizes]
    return pl.pallas_call(
        functools.partial(kernel, norm, chunks, n_copies),
        out_shape=(
            jax.ShapeDtypeStruct((w_rows, width), F32),
            jax.ShapeDtypeStruct((rows, channels // NY), BF16),
        ),
        in_specs=[pl.BlockSpec(memory_space=pltpu.HBM)] * 5,
        out_specs=(pl.BlockSpec(memory_space=pltpu.HBM),) * 2,
        scratch_shapes=scratch,
        compiler_params=pltpu.CompilerParams(
            collective_id=0, has_side_effects=True, vmem_limit_bytes=56 * 1024 * 1024
        ),
    )(tokens, gate_pre.T, hid_grad.T, up_weight, grad_accum)


def solution(mesh):
    fine = Mesh(mesh.devices.reshape(NY, NH, NC, NX, NL), ("y", "zh", "c", "x", "zl"))
    fsdp = ("y", "zh", "c")
    rows, both = P(fsdp, None), P(fsdp, ("x", "zl"))
    return jax.shard_map(
        on_device,
        mesh=fine,
        in_specs=(rows, both, both, both, both),
        out_specs=(both, both),
        check_vma=False,
    )
```

```python
import functools
import math

import jax
import jax.numpy as jnp
from jax import lax
from jax.experimental import pallas as pl
from jax.experimental.pallas import tpu as pltpu
from jax.sharding import Mesh, PartitionSpec as P

NY, NH, NC, NX, NL = 8, 4, 2, 4, 2
OFF = (0, 1, -1, 2, -2, 3, -3, 4)
BACK = (0, 2, 1, 4, 3, 6, 5, 7)
PLUS, MINUS = (0, 2, 4, 6, 7), (0, 1, 3, 5, 7)
TEAMS = ((0,), (1, 2), (3, 4), (5, 6), (7,))
SPLIT = (512, 1024, 1536)
F32, BF16 = jnp.float32, jnp.bfloat16
PLAN = (
    ("up", 0), ("enter",), ("ring", 0, 0, 0), ("w_send",), ("ring", 0, 1, 0), ("tok_send",),
    ("up", 1), ("up", 2), ("ring", 1, 1, 0), ("ring", 0, 1, 1), ("up", 3), ("ring", 2, 1, 0),
    ("ring", 1, 0, 0), ("tok_pair",), ("ring", 1, 1, 1), ("ring", 0, 0, 1), ("ring", 0, 1, 2),
    ("w_forward",), ("ring", 1, 0, 1), ("ring", 2, 0, 0), ("tok_spread",), ("ring", 1, 1, 2),
    ("ring", 0, 0, 2), ("ring", 1, 0, 2), ("ring", 3, 0, 0), ("w_share",), ("ring", 3, 1, 0),
    ("ring", 0, 1, 3), ("ring", 1, 1, 3), ("tok_forward",), ("ring", 0, 0, 3), ("w_ready",),
    ("p_begin", 0), ("p_send", 0), ("ring", 1, 0, 3), ("ring", 2, 0, 1), ("ring", 2, 1, 1),
    ("p_begin", 1), ("ring", 3, 0, 1), ("ring", 3, 1, 1), ("p_send", 1), ("got", 0, 1, 4),
    ("tok_turn",), ("got", 0, 0, 4), ("grad_other", 0), ("grad_own", 0), ("got", 1, 1, 4),
    ("got", 1, 0, 4), ("grad_other", 1), ("ring", 2, 0, 2), ("z_send", 0), ("grad_own", 1),
    ("ring", 2, 1, 2), ("z_send", 1), ("ring", 3, 1, 2), ("ring", 3, 0, 2), ("p_begin", 2),
    ("p_send", 2), ("ring", 2, 0, 3), ("z_mid", 0), ("ring", 2, 1, 3), ("p_end", 1), ("p_begin", 3),
    ("ring", 3, 1, 3), ("z_mid", 1), ("ring", 3, 0, 3), ("p_send", 3), ("p_end", 0),
    ("got", 2, 0, 4), ("got", 2, 1, 4), ("grad_other", 2), ("grad_own", 2), ("p_begin", 4),
    ("got", 3, 0, 4), ("got", 3, 1, 4), ("grad_other", 3), ("z_send", 2), ("p_send", 4),
    ("p_end", 2), ("grad_own", 3), ("z_send", 3), ("p_end", 3), ("p_end", 4), ("drain",),
    ("z_mid", 2), ("z_end", 0), ("z_end", 1), ("z_end", 3), ("z_end", 2),
)


def kernel(chunks, n_copies, tokens, gate_in, hid_in, w_own, wg_out, ig_out, *scratch):
    scratch = list(scratch)
    take = lambda n: [scratch.pop(0) for _ in range(n)]
    nk = len(chunks)
    send_sem, recv_sem, fin_send, fin_recv, load_sem = take(5)
    gate, hid, tok_own, tok, tok_t, w_all, fin = take(7)
    up = take(nk)
    b_send, b_recv, b_own, b_sum, b_l, b_r, b_f, b_up, b_down = (take(nk) for _ in range(9))
    nt = len(TEAMS)
    p_acc, p_all, p_l, p_r, p_f, p_fin = (take(nt) for _ in range(6))

    y, zh, c, x, zl = (lax.axis_index(a) for a in ("y", "zh", "c", "x", "zl"))
    zc, t = zh * NC + c, x * NL + zl
    around = lambda v, n: lax.rem(v + n, n)
    y_up, y_down = {"y": around(y + 1, NY)}, {"y": around(y - 1, NY)}
    h_up, h_down = around(zh + 1, NH), around(zh - 1, NH)
    h_far = around(zh + 2, NH)
    x_up, x_down, x_far = around(x + 1, NX), around(x - 1, NX), around(x + 2, NX)
    sib = {"c": 1 - c}
    fin_x, fin_l = y // NL, lax.rem(y, NL)
    MESH = pl.DeviceIdType.MESH

    copies = []

    def send(src, dst, device):
        i = len(copies)
        copy = pltpu.make_async_remote_copy(
            src_ref=src,
            dst_ref=dst,
            send_sem=send_sem.at[i],
            recv_sem=recv_sem.at[i],
            device_id=device,
            device_id_type=MESH,
        )
        copy.start()
        copies.append(copy)
        return copy

    def fin_copy(j, src, sem):
        return pltpu.make_async_remote_copy(
            src_ref=src,
            dst_ref=fin.at[x, zl],
            send_sem=fin_send.at[j],
            recv_sem=fin_recv.at[sem],
            device_id={"y": around(y + OFF[j], NY), "x": fin_x, "zl": fin_l},
            device_id_type=MESH,
        )

    loads = {}

    def load(name, src, dst):
        loads[name] = pltpu.make_async_copy(src, dst, load_sem.at[len(loads)])
        loads[name].start()

    def load_group(k):
        part = pl.ds(*chunks[k])
        load((0, k), gate_in.at[part], gate.at[part])
        load((1, k), hid_in.at[part], hid.at[part])

    load_group(0)

    barrier = pltpu.get_barrier_semaphore()

    def greet(device):
        pl.semaphore_signal(barrier, inc=1, device_id=device, device_id_type=MESH)

    for j in range(1, NY):
        greet({"y": around(y + OFF[j], NY)})
    for h in (h_up, h_down, h_far):
        greet({"zh": h})
    for v in (x_up, x_down, x_far):
        greet({"x": v})
    greet({"zl": 1 - zl})
    greet(sib)
    for other in range(NX * NL):

        @pl.when(jnp.logical_or(t != y, t != other))
        def _():
            greet({"y": t, "x": other // NL, "zl": other % NL})

    for k in range(1, nk):
        load_group(k)

    def load_rest():
        load("w", w_own, w_all.at[zc])
        columns = pl.ds(pl.multiple_of(y * 512, 512), 512)
        load("tok", tokens.at[:, columns], tok_own)

    def up_grad(k):
        loads[0, k].wait()
        loads[1, k].wait()
        at, width = chunks[k]
        v = gate[at : at + width].astype(F32)
        g = hid[at : at + width].astype(F32)
        up[k][0] = (g * (v / (1.0 + jnp.exp(-v)))).astype(BF16).T

    ring = {}

    def arrived(k, half, s):
        for way in (0, 1):
            if s < 4 or way == half:
                ring[k, half, s - 1, way].wait_recv()

    def ring_step(k, half, s):
        if s:
            arrived(k, half, s)
        rows = pl.ds(half * 64, 64)
        for way, path, device in ((0, PLUS, y_up), (1, MINUS, y_down)):
            if s < 3 or way == half:
                ring[k, half, s, way] = send(
                    up[k].at[path[s], rows], up[k].at[path[s + 1], rows], device
                )

    tok_in, tok_x = [], []
    others = pl.ds(1, NY - 1)

    def tok_send():
        for j in range(1, NY):
            to = around(y + OFF[j], NY)
            rows = pl.ds(pl.multiple_of(t * 16, 16), 16)
            columns = pl.ds(pl.multiple_of(to * 512, 512), 512)
            tok_in.append(send(tokens.at[rows, columns], tok.at[BACK[j], x, zl], {"y": to}))

    def tok_pair():
        for copy in tok_in:
            copy.wait_recv()
        eighth = tok.at[others, x, zl]
        tok_in.append(send(eighth, eighth, {"zl": 1 - zl}))

    def tok_spread():
        tok_in[NY - 1].wait_recv()
        quarter = tok.at[others, x]
        tok_x.append(send(quarter, quarter, {"x": x_up}))
        tok_x.append(send(quarter, quarter, {"x": x_down}))

    def tok_forward():
        tok_x[0].wait_recv()
        tok_x[1].wait_recv()
        a = tok.at[others, x_down, 0]
        b = tok.at[others, x_up, 1]
        tok_x.append(send(a, a, {"x": x_up}))
        tok_x.append(send(b, b, {"x": x_down}))

    def tok_turn():
        tok_x[2].wait_recv()
        tok_x[3].wait_recv()
        for j in range(NY):
            if j == 0:
                loads["tok"].wait()
                block = tok_own[...]
            else:
                block = tok[j].reshape(128, 512)
            turned = block.T
            for h in range(NH):
                for core in range(NC):
                    row = (h * NC + core) * 64
                    tok_t[core, h * 64 : h * 64 + 64, j * 128 : j * 128 + 128] = turned[row : row + 64]

    w_in = []

    def w_send():
        for device in ({"zh": h_up}, {"zh": h_down}, sib):
            w_in.append(send(w_own, w_all.at[zc], device))
        load_rest()

    def w_forward():
        w_in[0].wait_recv()
        w_in[1].wait_recv()
        left, right = h_down * NC + c, h_up * NC + c
        a, b = pl.ds(0, 32), pl.ds(32, 32)
        w_in.append(send(w_all.at[left, a], w_all.at[left, a], {"zh": h_up}))
        w_in.append(send(w_all.at[right, b], w_all.at[right, b], {"zh": h_down}))
        w_in.append(send(w_all.at[left], w_all.at[left], sib))
        w_in.append(send(w_all.at[right], w_all.at[right], sib))

    def w_share():
        far = h_far * NC + c
        w_in[3].wait_recv()
        w_in.append(send(w_all.at[far, pl.ds(0, 32)], w_all.at[far, pl.ds(0, 32)], sib))
        w_in[4].wait_recv()
        w_in.append(send(w_all.at[far, pl.ds(32, 32)], w_all.at[far, pl.ds(32, 32)], sib))

    def w_ready():
        loads["w"].wait()
        w_in[2].wait_recv()
        for copy in w_in[5:]:
            copy.wait_recv()

    share, zs = {}, {}

    def grad_part(k, core):
        ups = up[k][...].reshape(NY * 128, chunks[k][1])
        part = jnp.dot(tok_t[core], ups, preferred_element_type=F32)
        return part.reshape(NH, 64, chunks[k][1])

    def grad_other(k):
        b_send[k][...] = grad_part(k, 1 - c).astype(BF16)
        share[k] = send(b_send[k], b_recv[k], sib)

    def grad_own(k):
        b_own[k][...] = grad_part(k, c)

    def z_send(k):
        share[k].wait_recv()
        total = b_own[k][...] + b_recv[k][...].astype(F32)
        b_own[k][...] = total
        b_sum[k][...] = total.astype(BF16)
        if k == nk - 1:
            zs[k] = [
                send(b_sum[k].at[h], into[k], {"zh": h})
                for h, into in ((h_far, b_f), (h_up, b_l), (h_down, b_r))
            ]
        else:
            a, b = pl.ds(0, 32), pl.ds(32, 32)
            zs[k] = [
                send(b_sum[k].at[h_far, a], b_f[k].at[a], {"zh": h_up}),
                send(b_sum[k].at[h_far, b], b_f[k].at[b], {"zh": h_down}),
            ]

    def z_mid(k):
        zs[k][0].wait_recv()
        b_up[k][0:32] = (b_own[k][h_up, 0:32] + b_f[k][0:32].astype(F32)).astype(BF16)
        b_up[k][32:64] = b_own[k][h_up, 32:64].astype(BF16)
        zs[k].append(send(b_up[k], b_l[k], {"zh": h_up}))
        zs[k][1].wait_recv()
        b_down[k][0:32] = b_own[k][h_down, 0:32].astype(BF16)
        b_down[k][32:64] = (b_own[k][h_down, 32:64] + b_f[k][32:64].astype(F32)).astype(BF16)
        zs[k].append(send(b_down[k], b_r[k], {"zh": h_down}))

    def z_end(k):
        for copy in zs[k] if k == nk - 1 else zs[k][2:]:
            copy.wait_recv()
        total = b_own[k][zh]
        for other in (b_l, b_r, b_f) if k == nk - 1 else (b_l, b_r):
            total = total + other[k][...].astype(F32)
        at, width = chunks[k]
        wg_out[:, at : at + width] = total

    xs = {}

    def term(p, ks):
        first, n = TEAMS[p][0], len(TEAMS[p])
        total = None
        for k, cut in [(k, cut) for k in ks for cut in range(0, chunks[k][1], 512)]:
            at, width = chunks[k]
            end = min(cut + 512, width)
            lhs = up[k][first : first + n, :, cut:end].reshape(n * 128, end - cut)
            rhs = w_all[:, :, at + cut : at + end].reshape(NH * NC * 64, end - cut)
            one = lax.dot_general(lhs, rhs, (((1,), (1,)), ((), ())), preferred_element_type=F32)
            total = one if total is None else total + one
        return total

    def p_begin(p):
        p_acc[p][...] = term(p, range(nk - 1))

    def p_send(p):
        total = p_acc[p][...] + term(p, (nk - 1,))
        p_all[p][...] = total.astype(BF16).reshape(len(TEAMS[p]), NX, 32, 512)
        xs[p] = [
            send(p_all[p].at[:, v], into[p], {"x": v})
            for v, into in ((x_far, p_f), (x_up, p_l), (x_down, p_r))
        ]

    def p_end(p):
        for copy in xs[p]:
            copy.wait_recv()
        total = p_all[p][:, x].astype(F32)
        for other in (p_l, p_r, p_f):
            total = total + other[p][...].astype(F32)
        p_fin[p][...] = total.astype(BF16)
        for i, j in enumerate(TEAMS[p]):
            if j == 0:

                @pl.when(t == y)
                def _():
                    fin[x, zl] = p_fin[p][i]

                @pl.when(t != y)
                def _():
                    fin_copy(j, p_fin[p].at[i], t).start()

            else:
                fin_copy(j, p_fin[p].at[i], t).start()

    drained = []

    def drain():
        for copy in copies[len(drained) :]:
            copy.wait_send()
            drained.append(copy)

    def enter():
        pl.semaphore_wait(barrier, NY - 1 + 8 + jnp.where(t == y, NX * NL - 1, NX * NL))

    steps = {
        "enter": enter, "drain": drain, "up": up_grad, "ring": ring_step, "got": arrived,
        "tok_send": tok_send, "tok_pair": tok_pair, "tok_spread": tok_spread, "tok_forward": tok_forward, "tok_turn": tok_turn,
        "w_send": w_send, "w_forward": w_forward, "w_share": w_share, "w_ready": w_ready,
        "grad_other": grad_other, "grad_own": grad_own, "z_send": z_send, "z_mid": z_mid, "z_end": z_end,
        "p_begin": p_begin, "p_send": p_send, "p_end": p_end,
    }
    for step, *of in PLAN:
        steps[step](*of)

    for other in range(NX * NL):

        @pl.when(jnp.logical_or(t != y, t != other))
        def _():
            fin_copy(0, p_fin[0].at[0], other).wait_recv()

    ig_out[...] = fin[...]
    drain()
    assert len(copies) == n_copies

    @pl.when(t != y)
    def _():
        fin_copy(0, p_fin[0].at[0], t).wait_send()

    for p, team in enumerate(TEAMS):
        for i, j in enumerate(team):
            if j:
                fin_copy(j, p_fin[p].at[i], t).wait_send()


def on_device(tokens, gate_pre, hid_grad, up_weight, grad_accum):
    rows, channels = tokens.shape
    w_rows, width = up_weight.shape
    norm = 1.0 / math.sqrt(rows * NY * NH * NC)
    ends = (*SPLIT, width)
    chunks = [(at, end - at) for at, end in zip((0, *SPLIT), ends)]
    n_copies = 14 * len(chunks) + 8 + 4 + 9 + 5 * len(chunks) - 1 + 3 * len(TEAMS)
    dma, vmem = pltpu.SemaphoreType.DMA, pltpu.VMEM
    widths = [w for _, w in chunks]
    sizes = [len(team) for team in TEAMS]
    scratch = [dma((n_copies,)), dma((n_copies,)), dma((NY,)), dma((NX * NL,))]
    scratch += [dma((2 * len(chunks) + 2,))]
    scratch += [
        vmem((width, rows), BF16),
        vmem((width, rows), BF16),
        vmem((rows, 512), BF16),
        vmem((NY, NX, NL, 16, 512), BF16),
        vmem((NC, 256, 1024), BF16),
        vmem((NH * NC, w_rows, width), BF16),
        vmem((NX, NL, 32, 512), BF16),
    ]
    scratch += [vmem((NY, rows, w), BF16) for w in widths]
    for shape, kind in (
        ((NH, 64), BF16), ((NH, 64), BF16), ((NH, 64), F32), ((NH, 64), BF16),
        ((64,), BF16), ((64,), BF16), ((64,), BF16), ((64,), BF16), ((64,), BF16),
    ):
        scratch += [vmem((*shape, w), kind) for w in widths]
    scratch += [vmem((n * 128, 512), F32) for n in sizes]
    scratch += [vmem((n, NX, 32, 512), BF16) for n in sizes]
    for _ in range(4):
        scratch += [vmem((n, 32, 512), BF16) for n in sizes]
    in_hbm = lambda v: pltpu.with_memory_space_constraint(v, pltpu.HBM)
    total, parts = pl.pallas_call(
        functools.partial(kernel, chunks, n_copies),
        out_shape=(
            vmem((w_rows, width), F32),
            vmem((NX, NL, 32, channels // NY), BF16),
        ),
        in_specs=[pl.BlockSpec(memory_space=pltpu.HBM)] * 4,
        out_specs=(pl.BlockSpec(memory_space=pltpu.VMEM),) * 2,
        scratch_shapes=scratch,
        compiler_params=pltpu.CompilerParams(
            collective_id=0, has_side_effects=True, vmem_limit_bytes=48 * 1024 * 1024
        ),
    )(*(in_hbm(v) for v in (tokens, gate_pre.T, hid_grad.T, up_weight)))
    weight_grad = grad_accum + total * norm
    input_grad = (parts[:, 0].astype(F32) + parts[:, 1].astype(F32)).astype(BF16)
    return weight_grad, input_grad.reshape(rows, channels // NY)


def solution(mesh):
    fine = Mesh(mesh.devices.reshape(NY, NH, NC, NX, NL), ("y", "zh", "c", "x", "zl"))
    fsdp = ("y", "zh", "c")
    rows, both = P(fsdp, None), P(fsdp, ("x", "zl"))
    return jax.shard_map(
        on_device,
        mesh=fine,
        in_specs=(rows, both, both, both, both),
        out_specs=(both, both),
        check_vma=False,
    )
```

```python
import functools
import math

import jax
import jax.numpy as jnp
from jax import lax
from jax.experimental import pallas as pl
from jax.experimental.pallas import tpu as pltpu
from jax.sharding import Mesh, PartitionSpec as P

NY, NH, NC, NX, NL = 8, 4, 2, 4, 2
OFF = (0, 1, -1, 2, -2, 3, -3, 4)
BACK = (0, 2, 1, 4, 3, 6, 5, 7)
PLUS, MINUS = (0, 2, 4, 6, 7), (0, 1, 3, 5, 7)
TEAMS = ((0,), (1, 2), (3, 4), (5, 6), (7,))
SPLIT = (640, 1152, 1536)
F32, BF16 = jnp.float32, jnp.bfloat16
PLAN = (
    ("up", 0), ("enter",), ("ring", 0, 0, 0), ("w_send",), ("tok_send",), ("up", 1), ("up", 2),
    ("ring", 2, 1, 0), ("up", 3), ("ring", 3, 0, 0), ("ring", 0, 1, 0), ("ring", 2, 0, 0),
    ("ring", 1, 0, 0), ("ring", 0, 0, 1), ("tok_pair",), ("ring", 0, 1, 1), ("ring", 2, 1, 1),
    ("ring", 2, 0, 1), ("w_forward",), ("ring", 0, 0, 2), ("ring", 1, 1, 0), ("tok_spread",),
    ("ring", 0, 1, 2), ("ring", 2, 1, 2), ("ring", 2, 0, 2), ("ring", 0, 0, 3), ("ring", 3, 1, 0),
    ("w_share",), ("tok_forward",), ("w_ready",), ("p_begin", 0), ("p_send", 0), ("ring", 0, 1, 3),
    ("ring", 1, 1, 1), ("ring", 1, 0, 1), ("ring", 2, 0, 3), ("ring", 3, 0, 1), ("ring", 2, 1, 3),
    ("p_begin", 1), ("ring", 3, 1, 1), ("tok_turn",), ("got", 0, 0, 4), ("got", 0, 1, 4),
    ("grad_other", 0), ("p_send", 1), ("ring", 1, 1, 2), ("grad_own", 0), ("z_send", 0),
    ("ring", 1, 0, 2), ("p_begin", 2), ("ring", 3, 0, 2), ("got", 2, 1, 4), ("got", 2, 0, 4),
    ("grad_other", 2), ("ring", 3, 1, 2), ("p_send", 2), ("grad_own", 2), ("z_send", 2),
    ("ring", 1, 1, 3), ("z_mid", 0), ("ring", 1, 0, 3), ("p_begin", 3), ("ring", 3, 0, 3),
    ("p_end", 0), ("ring", 3, 1, 3), ("p_end", 1), ("p_send", 3), ("z_mid", 2), ("p_end", 2),
    ("got", 1, 1, 4), ("got", 1, 0, 4), ("grad_other", 1), ("grad_own", 1), ("p_begin", 4),
    ("got", 3, 1, 4), ("got", 3, 0, 4), ("grad_other", 3), ("z_send", 1), ("p_send", 4),
    ("grad_own", 3), ("z_send", 3), ("p_end", 3), ("z_end", 0), ("p_end", 4), ("drain",),
    ("z_end", 2), ("z_mid", 1), ("z_end", 3), ("z_end", 1),
)


def kernel(chunks, n_copies, tokens, gate_in, hid_in, w_own, wg_out, ig_out, *scratch):
    scratch = list(scratch)
    take = lambda n: [scratch.pop(0) for _ in range(n)]
    nk = len(chunks)
    send_sem, recv_sem, fin_send, fin_recv, load_sem = take(5)
    gate, hid, tok_own, tok, tok_t, w_all, fin = take(7)
    up = take(nk)
    b_send, b_recv, b_own, b_sum, b_l, b_r, b_f, b_up, b_down = (take(nk) for _ in range(9))
    nt = len(TEAMS)
    p_acc, p_all, p_l, p_r, p_f, p_fin = (take(nt) for _ in range(6))

    y, zh, c, x, zl = (lax.axis_index(a) for a in ("y", "zh", "c", "x", "zl"))
    zc, t = zh * NC + c, x * NL + zl
    around = lambda v, n: lax.rem(v + n, n)
    y_up, y_down = {"y": around(y + 1, NY)}, {"y": around(y - 1, NY)}
    h_up, h_down = around(zh + 1, NH), around(zh - 1, NH)
    h_far = around(zh + 2, NH)
    x_up, x_down, x_far = around(x + 1, NX), around(x - 1, NX), around(x + 2, NX)
    sib = {"c": 1 - c}
    fin_x, fin_l = y // NL, lax.rem(y, NL)
    MESH = pl.DeviceIdType.MESH

    copies = []

    def send(src, dst, device):
        i = len(copies)
        copy = pltpu.make_async_remote_copy(
            src_ref=src,
            dst_ref=dst,
            send_sem=send_sem.at[i],
            recv_sem=recv_sem.at[i],
            device_id=device,
            device_id_type=MESH,
        )
        copy.start()
        copies.append(copy)
        return copy

    def fin_copy(j, src, sem):
        return pltpu.make_async_remote_copy(
            src_ref=src,
            dst_ref=fin.at[x, zl],
            send_sem=fin_send.at[j],
            recv_sem=fin_recv.at[sem],
            device_id={"y": around(y + OFF[j], NY), "x": fin_x, "zl": fin_l},
            device_id_type=MESH,
        )

    loads = {}

    def load(name, src, dst):
        loads[name] = pltpu.make_async_copy(src, dst, load_sem.at[len(loads)])
        loads[name].start()

    def load_group(k):
        part = pl.ds(*chunks[k])
        load((0, k), gate_in.at[part], gate.at[part])
        load((1, k), hid_in.at[part], hid.at[part])

    load_group(0)

    barrier = pltpu.get_barrier_semaphore()

    def greet(device):
        pl.semaphore_signal(barrier, inc=1, device_id=device, device_id_type=MESH)

    for j in range(1, NY):
        greet({"y": around(y + OFF[j], NY)})
    for h in (h_up, h_down, h_far):
        greet({"zh": h})
    for v in (x_up, x_down, x_far):
        greet({"x": v})
    greet({"zl": 1 - zl})
    greet(sib)
    for other in range(NX * NL):

        @pl.when(jnp.logical_or(t != y, t != other))
        def _():
            greet({"y": t, "x": other // NL, "zl": other % NL})

    for k in range(1, nk):
        load_group(k)

    def load_rest():
        load("w", w_own, w_all.at[zc])
        columns = pl.ds(pl.multiple_of(y * 512, 512), 512)
        load("tok", tokens.at[:, columns], tok_own)

    def up_grad(k):
        loads[0, k].wait()
        loads[1, k].wait()
        at, width = chunks[k]
        v = gate[at : at + width].astype(F32)
        g = hid[at : at + width].astype(F32)
        up[k][0] = (g * (v / (1.0 + jnp.exp(-v)))).astype(BF16).T

    ring = {}

    def arrived(k, half, s):
        for way in (0, 1):
            if s < 4 or way == half:
                ring[k, half, s - 1, way].wait_recv()

    def ring_step(k, half, s):
        if s:
            arrived(k, half, s)
        rows = pl.ds(half * 64, 64)
        for way, path, device in ((0, PLUS, y_up), (1, MINUS, y_down)):
            if s < 3 or way == half:
                ring[k, half, s, way] = send(
                    up[k].at[path[s], rows], up[k].at[path[s + 1], rows], device
                )

    tok_in, tok_x = [], []
    others = pl.ds(1, NY - 1)

    def tok_send():
        for j in range(1, NY):
            to = around(y + OFF[j], NY)
            rows = pl.ds(pl.multiple_of(t * 16, 16), 16)
            columns = pl.ds(pl.multiple_of(to * 512, 512), 512)
            tok_in.append(send(tokens.at[rows, columns], tok.at[BACK[j], x, zl], {"y": to}))

    def tok_pair():
        for copy in tok_in:
            copy.wait_recv()
        eighth = tok.at[others, x, zl]
        tok_in.append(send(eighth, eighth, {"zl": 1 - zl}))

    def tok_spread():
        tok_in[NY - 1].wait_recv()
        quarter = tok.at[others, x]
        tok_x.append(send(quarter, quarter, {"x": x_up}))
        tok_x.append(send(quarter, quarter, {"x": x_down}))

    def tok_forward():
        tok_x[0].wait_recv()
        tok_x[1].wait_recv()
        a = tok.at[others, x_down, 0]
        b = tok.at[others, x_up, 1]
        tok_x.append(send(a, a, {"x": x_up}))
        tok_x.append(send(b, b, {"x": x_down}))

    def tok_turn():
        tok_x[2].wait_recv()
        tok_x[3].wait_recv()
        for j in range(NY):
            if j == 0:
                loads["tok"].wait()
                block = tok_own[...]
            else:
                block = tok[j].reshape(128, 512)
            turned = block.T
            for h in range(NH):
                for core in range(NC):
                    row = (h * NC + core) * 64
                    tok_t[core, h * 64 : h * 64 + 64, j * 128 : j * 128 + 128] = turned[row : row + 64]

    w_in = []

    def w_send():
        for device in ({"zh": h_up}, {"zh": h_down}, sib):
            w_in.append(send(w_own, w_all.at[zc], device))
        load_rest()

    def w_forward():
        w_in[0].wait_recv()
        w_in[1].wait_recv()
        left, right = h_down * NC + c, h_up * NC + c
        a, b = pl.ds(0, 32), pl.ds(32, 32)
        w_in.append(send(w_all.at[left, a], w_all.at[left, a], {"zh": h_up}))
        w_in.append(send(w_all.at[right, b], w_all.at[right, b], {"zh": h_down}))
        w_in.append(send(w_all.at[left], w_all.at[left], sib))
        w_in.append(send(w_all.at[right], w_all.at[right], sib))

    def w_share():
        far = h_far * NC + c
        w_in[3].wait_recv()
        w_in.append(send(w_all.at[far, pl.ds(0, 32)], w_all.at[far, pl.ds(0, 32)], sib))
        w_in[4].wait_recv()
        w_in.append(send(w_all.at[far, pl.ds(32, 32)], w_all.at[far, pl.ds(32, 32)], sib))

    def w_ready():
        loads["w"].wait()
        w_in[2].wait_recv()
        for copy in w_in[5:]:
            copy.wait_recv()

    share, zs = {}, {}

    def grad_part(k, core):
        ups = up[k][...].reshape(NY * 128, chunks[k][1])
        part = jnp.dot(tok_t[core], ups, preferred_element_type=F32)
        return part.reshape(NH, 64, chunks[k][1])

    def grad_other(k):
        b_send[k][...] = grad_part(k, 1 - c).astype(BF16)
        share[k] = send(b_send[k], b_recv[k], sib)

    def grad_own(k):
        b_own[k][...] = grad_part(k, c)

    def z_send(k):
        share[k].wait_recv()
        total = b_own[k][...] + b_recv[k][...].astype(F32)
        b_own[k][...] = total
        b_sum[k][...] = total.astype(BF16)
        if k == nk - 1:
            zs[k] = [
                send(b_sum[k].at[h], into[k], {"zh": h})
                for h, into in ((h_far, b_f), (h_up, b_l), (h_down, b_r))
            ]
        else:
            a, b = pl.ds(0, 32), pl.ds(32, 32)
            zs[k] = [
                send(b_sum[k].at[h_far, a], b_f[k].at[a], {"zh": h_up}),
                send(b_sum[k].at[h_far, b], b_f[k].at[b], {"zh": h_down}),
            ]

    def z_mid(k):
        zs[k][0].wait_recv()
        b_up[k][0:32] = (b_own[k][h_up, 0:32] + b_f[k][0:32].astype(F32)).astype(BF16)
        b_up[k][32:64] = b_own[k][h_up, 32:64].astype(BF16)
        zs[k].append(send(b_up[k], b_l[k], {"zh": h_up}))
        zs[k][1].wait_recv()
        b_down[k][0:32] = b_own[k][h_down, 0:32].astype(BF16)
        b_down[k][32:64] = (b_own[k][h_down, 32:64] + b_f[k][32:64].astype(F32)).astype(BF16)
        zs[k].append(send(b_down[k], b_r[k], {"zh": h_down}))

    def z_end(k):
        for copy in zs[k] if k == nk - 1 else zs[k][2:]:
            copy.wait_recv()
        total = b_own[k][zh]
        for other in (b_l, b_r, b_f) if k == nk - 1 else (b_l, b_r):
            total = total + other[k][...].astype(F32)
        at, width = chunks[k]
        wg_out[:, at : at + width] = total

    xs = {}

    def term(p, ks):
        first, n = TEAMS[p][0], len(TEAMS[p])
        total = None
        for k, cut in [(k, cut) for k in ks for cut in range(0, chunks[k][1], 512)]:
            at, width = chunks[k]
            end = min(cut + 512, width)
            lhs = up[k][first : first + n, :, cut:end].reshape(n * 128, end - cut)
            rhs = w_all[:, :, at + cut : at + end].reshape(NH * NC * 64, end - cut)
            one = lax.dot_general(lhs, rhs, (((1,), (1,)), ((), ())), preferred_element_type=F32)
            total = one if total is None else total + one
        return total

    def p_begin(p):
        p_acc[p][...] = term(p, range(nk - 1))

    def p_send(p):
        total = p_acc[p][...] + term(p, (nk - 1,))
        p_all[p][...] = total.astype(BF16).reshape(len(TEAMS[p]), NX, 32, 512)
        xs[p] = [
            send(p_all[p].at[:, v], into[p], {"x": v})
            for v, into in ((x_far, p_f), (x_up, p_l), (x_down, p_r))
        ]

    def p_end(p):
        for copy in xs[p]:
            copy.wait_recv()
        total = p_all[p][:, x].astype(F32)
        for other in (p_l, p_r, p_f):
            total = total + other[p][...].astype(F32)
        p_fin[p][...] = total.astype(BF16)
        for i, j in enumerate(TEAMS[p]):
            if j == 0:

                @pl.when(t == y)
                def _():
                    fin[x, zl] = p_fin[p][i]

                @pl.when(t != y)
                def _():
                    fin_copy(j, p_fin[p].at[i], t).start()

            else:
                fin_copy(j, p_fin[p].at[i], t).start()

    drained = []

    def drain():
        for copy in copies[len(drained) :]:
            copy.wait_send()
            drained.append(copy)

    def enter():
        pl.semaphore_wait(barrier, NY - 1 + 8 + jnp.where(t == y, NX * NL - 1, NX * NL))

    steps = {
        "enter": enter, "drain": drain, "up": up_grad, "ring": ring_step, "got": arrived,
        "tok_send": tok_send, "tok_pair": tok_pair, "tok_spread": tok_spread, "tok_forward": tok_forward, "tok_turn": tok_turn,
        "w_send": w_send, "w_forward": w_forward, "w_share": w_share, "w_ready": w_ready,
        "grad_other": grad_other, "grad_own": grad_own, "z_send": z_send, "z_mid": z_mid, "z_end": z_end,
        "p_begin": p_begin, "p_send": p_send, "p_end": p_end,
    }
    for step, *of in PLAN:
        steps[step](*of)

    for other in range(NX * NL):

        @pl.when(jnp.logical_or(t != y, t != other))
        def _():
            fin_copy(0, p_fin[0].at[0], other).wait_recv()

    ig_out[...] = fin[...]
    drain()
    assert len(copies) == n_copies

    @pl.when(t != y)
    def _():
        fin_copy(0, p_fin[0].at[0], t).wait_send()

    for p, team in enumerate(TEAMS):
        for i, j in enumerate(team):
            if j:
                fin_copy(j, p_fin[p].at[i], t).wait_send()


def on_device(tokens, gate_pre, hid_grad, up_weight, grad_accum):
    rows, channels = tokens.shape
    w_rows, width = up_weight.shape
    norm = 1.0 / math.sqrt(rows * NY * NH * NC)
    ends = (*SPLIT, width)
    chunks = [(at, end - at) for at, end in zip((0, *SPLIT), ends)]
    n_copies = 14 * len(chunks) + 8 + 4 + 9 + 5 * len(chunks) - 1 + 3 * len(TEAMS)
    dma, vmem = pltpu.SemaphoreType.DMA, pltpu.VMEM
    widths = [w for _, w in chunks]
    sizes = [len(team) for team in TEAMS]
    scratch = [dma((n_copies,)), dma((n_copies,)), dma((NY,)), dma((NX * NL,))]
    scratch += [dma((2 * len(chunks) + 2,))]
    scratch += [
        vmem((width, rows), BF16),
        vmem((width, rows), BF16),
        vmem((rows, 512), BF16),
        vmem((NY, NX, NL, 16, 512), BF16),
        vmem((NC, 256, 1024), BF16),
        vmem((NH * NC, w_rows, width), BF16),
        vmem((NX, NL, 32, 512), BF16),
    ]
    scratch += [vmem((NY, rows, w), BF16) for w in widths]
    for shape, kind in (
        ((NH, 64), BF16), ((NH, 64), BF16), ((NH, 64), F32), ((NH, 64), BF16),
        ((64,), BF16), ((64,), BF16), ((64,), BF16), ((64,), BF16), ((64,), BF16),
    ):
        scratch += [vmem((*shape, w), kind) for w in widths]
    scratch += [vmem((n * 128, 512), F32) for n in sizes]
    scratch += [vmem((n, NX, 32, 512), BF16) for n in sizes]
    for _ in range(4):
        scratch += [vmem((n, 32, 512), BF16) for n in sizes]
    in_hbm = lambda v: pltpu.with_memory_space_constraint(v, pltpu.HBM)
    total, parts = pl.pallas_call(
        functools.partial(kernel, chunks, n_copies),
        out_shape=(
            vmem((w_rows, width), F32),
            vmem((NX, NL, 32, channels // NY), BF16),
        ),
        in_specs=[pl.BlockSpec(memory_space=pltpu.HBM)] * 4,
        out_specs=(pl.BlockSpec(memory_space=pltpu.VMEM),) * 2,
        scratch_shapes=scratch,
        compiler_params=pltpu.CompilerParams(
            collective_id=0, has_side_effects=True, vmem_limit_bytes=48 * 1024 * 1024
        ),
    )(*(in_hbm(v) for v in (tokens, gate_pre.T, hid_grad.T, up_weight)))
    weight_grad = grad_accum + total * norm
    input_grad = (parts[:, 0].astype(F32) + parts[:, 1].astype(F32)).astype(BF16)
    return weight_grad, input_grad.reshape(rows, channels // NY)


def solution(mesh):
    fine = Mesh(mesh.devices.reshape(NY, NH, NC, NX, NL), ("y", "zh", "c", "x", "zl"))
    fsdp = ("y", "zh", "c")
    rows, both = P(fsdp, None), P(fsdp, ("x", "zl"))
    return jax.shard_map(
        on_device,
        mesh=fine,
        in_specs=(rows, both, both, both, both),
        out_specs=(both, both),
        check_vma=False,
    )
```
